32 devices in a mesh: groups: 2 (over x), ep: 16 (over z, y, core).
Axes of the slice: x: 2, y: 2, z: 4, core: 2. Of those that a mesh axis runs over, the one named last changes fastest.
Arguments:
- resid: bfloat16 [128, 3584], P(('groups', 'ep')), parts along dimension 0, may hold values from -45 to 45
- q_latent: bfloat16 [128, 16, 512], P(('groups', 'ep')), parts along dimension 0, may hold values from -500 to 500
- q_rope: bfloat16 [128, 16, 64], P(('groups', 'ep')), parts along dimension 0, may hold values from -6 to 6
- cache_latent: bfloat16 [128, 1024, 512], P(('groups', 'ep')), parts along dimension 0, may hold values from -4 to 4
- cache_rope: bfloat16 [128, 64, 1024], P(('groups', 'ep')), parts along dimension 0, may hold values from -4 to 4
- lengths: int32 [128], P(('groups', 'ep')), parts along dimension 0, may hold values from 2 to 1024, as said below
- w_value: bfloat16 [16, 512, 128], P('ep'), may hold values from -0.25 to 0.25
- w_out: bfloat16 [2048, 3584], P('ep'), may hold values from -0.125 to 0.125
- norm_gain: float32 [3584], replicated, may hold values from 0.1 to 1.9
- routes: int32 [128, 8], P(('groups', 'ep')), parts along dimension 0, may hold values from 0 to 15, all different within a row; in each aligned block of 4 rows (0 to 3, 4 to 7, ...) at most 2 rows name the same one
- route_scores: float32 [128, 8], P(('groups', 'ep')), parts along dimension 0, may hold values from 0.05 to 1
- placement: int32 [32], P('groups'), parts along dimension 0, may hold values from 0 to 15, each once
- w_gate: bfloat16 [16384, 3584], P('ep'), may hold values from -0.09375 to 0.09375
- w_up: bfloat16 [16384, 3584], P('ep'), may hold values from -0.09375 to 0.09375
- w_down: bfloat16 [16384, 3584], P('ep'), may hold values from -0.1875 to 0.1875
Outputs:
- mixed: bfloat16 [128, 3584], P(('groups', 'ep')), parts along dimension 0
The draws below stay inside these ranges and needn't reach their ends.
There are 2 independent parts, one for each index of `groups`. The reference program is written for one: setup_inputs(seed, part) draws one part's arguments, and reference() takes and returns one part's arrays. A program takes and returns all parts, laid end to end along the dimension named above; an argument that names none is the same for every part. Nothing has to cross between parts.
Inputs may be any that keep to these rules, and one draw needn't show every extreme that they name: `routes`: each row names 8 different experts; in the rows of one device (aligned blocks of 4 rows) every expert is named by exactly 2 rows. `placement`: each expert has its own slot. Positions 0 to lengths[r] - 1 of row r are live; some row is live over all 1024 positions.
All inputs are finite; a program needn't handle non-finite values.
Results may differ from the reference program's by a relative error of at most 0.0045.
Values may be sent and summed in bfloat16 or wider, within the bound.
A program may use at most 128 MiB of HBM per device.

```python
import math
import jax
import jax.numpy as jnp
import numpy as np
from jax import lax

D = 3584
FF = 1024
LAT = 512
ROPE = 64
VHEAD = 128
EXPERTS = 16
TOPK = 8
ROWS_DEV = 4
LEN = 1024
HEADS = 16
ROWS = 64
CAP = 2


def first_keys(key):
    return jnp.clip(jax.random.normal(jax.random.fold_in(key, 500), (ROWS, 2, LAT), jnp.float32), -4.0, 4.0)


def draw_cache_latent(key, part):
    base = first_keys(key)
    key = jax.random.fold_in(key, 1)
    rest = jnp.clip(jax.random.normal(key, (ROWS, LEN, LAT), jnp.float32), -4.0, 4.0)
    whole = jnp.concatenate([base, rest[:, 2:, :]], axis=1)
    return whole.astype(jnp.bfloat16)


def draw_q_latent(key, part):
    key = jax.random.fold_in(key, 2)
    key_drawn = jax.random.fold_in(key, 0)
    drawn = jnp.clip(jax.random.normal(key_drawn, (ROWS, HEADS, LAT), jnp.float32), -5.0, 5.0)
    return drawn.astype(jnp.bfloat16)


def draw_resid(key, part):
    key = jax.random.fold_in(key, 4)
    column = jnp.arange(D, dtype=jnp.float32) / D
    values = jnp.clip(jax.random.normal(key, (ROWS, D), jnp.float32), -5.0, 5.0) * (3.0 ** column)[None, :]
    return values.astype(jnp.bfloat16)


def draw_lengths(key, part):
    key = jax.random.fold_in(key, 6)
    key_a, key_b, key_c = jax.random.split(key, 3)
    first = jax.random.randint(key_a, (ROWS,), 1, LEN + 1)
    second = jax.random.randint(key_b, (ROWS,), 1, LEN + 1)
    lens = jnp.maximum(2, first * second // LEN)
    full = jax.random.randint(key_c, (), 0, ROWS)
    return jnp.where(jnp.arange(ROWS) == full, LEN, lens).astype(jnp.int32)


def block_levels(key, extent, cuts, smallest, top_value):
    loudness, own = 1.0, jax.random.fold_in(key, 6)
    for dim, blocks in cuts:
        draws = jnp.exp(jax.random.uniform(jax.random.fold_in(own, dim), (blocks,), jnp.float32, smallest / len(cuts), top_value / len(cuts)))
        loudness = loudness * jnp.repeat(draws, extent[dim] // blocks).reshape([-1 if axis == dim else 1 for axis in range(len(extent))])
    return loudness


def deal_out(own_key, own, number, rows, number_of, top, reach, lean):
    ranking = jax.random.permutation(own_key, number_of)
    crowded, usual = portions_of(number_of, rows * top, reach, lean, True), portions_of(number_of, rows * top, reach, lean, False)
    places = jnp.arange(number_of)

    def named(sizes, rotation):
        used = int((sizes > 0).sum())
        fixed = max(1, used // 4)
        shifted = fixed + (places - fixed + rotation * (used - fixed)) % max(1, number_of - fixed)
        return jnp.zeros((number_of,), jnp.int32).at[ranking[jnp.where(places < fixed, places, shifted)]].set(jnp.asarray(sizes, jnp.int32))

    sizes = jnp.where(number % 4 == 0, named(crowded, number // 4), named(usual, number - number // 4 - 1))
    mixed = jax.random.permutation(jax.random.fold_in(own, 3), number_of)
    giver, taker = mixed[0:number_of // 2 * 2:2], mixed[1:number_of // 2 * 2:2]
    slack = jnp.minimum(sizes[giver] - 1, reach - sizes[taker]) // 2
    slack = jnp.where((giver == ranking[0]) | (taker == ranking[0]) | (sizes[taker] == 0), 0, jnp.maximum(slack, 0))
    shifted = jax.random.randint(jax.random.fold_in(own, 4), (number_of // 2,), 0, 1 << 20) % (slack + 1)
    sizes = sizes.at[giver].add(-shifted).at[taker].add(shifted)
    labels = jnp.searchsorted(jnp.cumsum(sizes), jnp.arange(rows * top), side="right").astype(jnp.int32)
    table = labels.reshape(top, rows).T
    table = table[jax.random.permutation(jax.random.fold_in(own, 1), rows)]
    rotation = jax.random.randint(jax.random.fold_in(own, 2), (rows, 1), 0, top)
    return jnp.take_along_axis(table, (jnp.arange(top)[None, :] + rotation) % top, axis=1)


def portions_of(count, total, bound, skew, full):
    portions = [(1 << 20) // math.isqrt(rank ** skew) + 1 for rank in range(1, count + 1)]
    largest = bound if full else min(bound, max(-(-total // count), total * portions[0] // sum(portions)))
    least = 1 if total - largest >= count - 1 else 0
    holding, spare = [largest] + [least] * (count - 1), total - largest - least * (count - 1)
    while spare > 0:
        movable = [i for i in range(1, count) if holding[i] < largest] or [i for i in range(1, count) if holding[i] < bound]
        pool, left = sum([portions[i] for i in movable]), spare
        for i in movable:
            addition = min(bound - holding[i], max(1, left * portions[i] // pool), spare)
            holding[i] = holding[i] + addition
            spare = spare - addition
    return np.array(holding)


def centred(rng, extent, scale, reach, pieces=(), held_as=jnp.bfloat16):
    entries = scale * jax.random.normal(rng, extent, jnp.float32)
    if pieces:
        entries = entries * block_levels(rng, extent, pieces, -0.22, 0.18)
    return jnp.clip(entries, -reach, reach).astype(held_as)


def setup_inputs(seed: int = 0, part: int = 0) -> dict:
    streams_of = jax.random.split(jax.random.key(seed), 16)
    part_keys = jax.random.split(jax.random.fold_in(streams_of[15], part), 16)
    resid = draw_resid(jax.random.fold_in(jax.random.fold_in(streams_of[15], part), 71), part)
    q_latent = draw_q_latent(jax.random.fold_in(jax.random.fold_in(streams_of[15], part), 71), part)
    q_rope = centred(part_keys[2], (ROWS, HEADS, ROPE), 1.5, 6.0, ((0, 16),))
    cache_latent = draw_cache_latent(jax.random.fold_in(jax.random.fold_in(streams_of[15], part), 71), part)
    cache_rope = centred(part_keys[4], (ROWS, ROPE, LEN), 1.0, 4.0, ((0, 16),))
    lengths = draw_lengths(jax.random.fold_in(jax.random.fold_in(streams_of[15], part), 71), part)
    w_value = centred(streams_of[6], (HEADS, LAT, VHEAD), LAT ** -0.5, 0.25, ((0, 16),))
    w_out = centred(streams_of[7], (HEADS * VHEAD, D), (HEADS * VHEAD) ** -0.5, 0.125, ((0, 16),))
    norm_gain = jnp.clip(1.0 + 0.18 * jax.random.normal(streams_of[8], (D,), jnp.float32), 0.1, 1.9)
    routes_keys = jax.random.split(jax.random.fold_in(part_keys[9], 1), ROWS // ROWS_DEV)
    routes_turns = jax.random.permutation(jax.random.fold_in(part_keys[9], 3), ROWS // ROWS_DEV)
    routes = jax.vmap(lambda own, number: deal_out(jax.random.fold_in(part_keys[9], 2), own, number, ROWS_DEV, EXPERTS, TOPK, CAP, 0))(routes_keys, routes_turns).reshape((ROWS, TOPK))
    route_scores = jnp.clip(jnp.exp(math.log(1.0) - 2.9957323 * jax.random.uniform(part_keys[10], (ROWS, TOPK), jnp.float32) ** block_levels(part_keys[10], (ROWS, TOPK), ((0, 16),), -0.2, 0.2)), 0.05, 1.0)
    placement = jax.random.permutation(part_keys[11], EXPERTS).astype(jnp.int32)
    w_gate = centred(streams_of[12], (EXPERTS * FF, D), D ** -0.5, 0.09375, ((0, 16),))
    w_up = centred(streams_of[13], (EXPERTS * FF, D), D ** -0.5, 0.09375, ((0, 16),))
    w_down = centred(streams_of[14], (EXPERTS * FF, D), FF ** -0.5, 0.1875, ((0, 16),))
    return dict(resid=resid, q_latent=q_latent, q_rope=q_rope, cache_latent=cache_latent, cache_rope=cache_rope, lengths=lengths, w_value=w_value, w_out=w_out, norm_gain=norm_gain, routes=routes, route_scores=route_scores, placement=placement, w_gate=w_gate, w_up=w_up, w_down=w_down)


def attend_block(block):
    q_lat, q_rot, c_lat, c_rot, live = block
    scale = (VHEAD + ROPE) ** (-0.5)
    scores = jnp.einsum('rhc,rpc->rhp', q_lat.astype(jnp.float32), c_lat.astype(jnp.float32))
    scores = scores + jnp.einsum('rhk,rkp->rhp', q_rot.astype(jnp.float32), c_rot.astype(jnp.float32))
    scores = scores * scale
    valid = jnp.arange(LEN, dtype=jnp.int32)[None, None, :] < live[:, None, None]
    scores = jnp.where(valid, scores, -1e+30)
    top = lax.optimization_barrier(jnp.max(scores, axis=-1, keepdims=True))
    expo = jnp.where(valid, jnp.exp(scores - top), 0.0)
    probs = (expo / lax.optimization_barrier(jnp.sum(expo, axis=-1, keepdims=True))).astype(jnp.bfloat16)
    return jnp.einsum('rhp,rpc->rhc', probs.astype(jnp.float32), c_lat.astype(jnp.float32)).astype(jnp.bfloat16)

def reference(resid, q_latent, q_rope, cache_latent, cache_rope, lengths, w_value, w_out, norm_gain, routes, route_scores, placement, w_gate, w_up, w_down):
    blocks = ROWS // ROWS_DEV
    o_latent = lax.map(attend_block, (q_latent.reshape(blocks, ROWS_DEV, HEADS, LAT), q_rope.reshape(blocks, ROWS_DEV, HEADS, ROPE), cache_latent.reshape(blocks, ROWS_DEV, LEN, LAT), cache_rope.reshape(blocks, ROWS_DEV, ROPE, LEN), lengths.reshape(blocks, ROWS_DEV)))
    o_latent = o_latent.reshape(ROWS, HEADS, LAT)
    values = jnp.einsum('rhc,hcv->rhv', o_latent.astype(jnp.float32), w_value.astype(jnp.float32)).astype(jnp.bfloat16)
    attn = jnp.dot(values.reshape(ROWS, HEADS * VHEAD), w_out, preferred_element_type=jnp.float32)
    hidden = resid.astype(jnp.float32) + attn
    mean_sq = lax.optimization_barrier(jnp.mean(hidden * hidden, axis=-1, keepdims=True))
    normed = (hidden * lax.rsqrt(mean_sq + 1e-06) * norm_gain).astype(jnp.bfloat16)
    weights = 2.5 * route_scores / lax.optimization_barrier(jnp.sum(route_scores, axis=-1, keepdims=True))
    flat_ids = routes.reshape(-1)
    order = jnp.argsort(flat_ids, stable=True).astype(jnp.int32)
    per_expert = ROWS * TOPK // EXPERTS
    src_rows = (order // TOPK).reshape(EXPERTS, per_expert)

    def expert_out(index):
        taken = normed[src_rows[index]]
        start = (placement[index] * FF).astype(jnp.int32)
        gate_rows = lax.dynamic_slice_in_dim(w_gate, start, FF, 0)
        up_rows = lax.dynamic_slice_in_dim(w_up, start, FF, 0)
        down_rows = lax.dynamic_slice_in_dim(w_down, start, FF, 0)
        gate = jnp.dot(taken, gate_rows.T, preferred_element_type=jnp.float32)
        up = jnp.dot(taken, up_rows.T, preferred_element_type=jnp.float32)
        act = (jax.nn.silu(gate) * up).astype(jnp.bfloat16)
        return jnp.dot(act, down_rows, preferred_element_type=jnp.float32)
    outs = lax.map(expert_out, jnp.arange(EXPERTS, dtype=jnp.int32))
    pair_out = jnp.zeros((ROWS * TOPK, D), jnp.float32).at[order].set(outs.reshape(-1, D))
    moe = lax.optimization_barrier(jnp.sum(weights[:, :, None] * pair_out.reshape(ROWS, TOPK, D), axis=1))
    return (hidden + moe).astype(jnp.bfloat16)
```

```python
import jax
import jax.numpy as jnp
from jax import lax
from jax.sharding import PartitionSpec as P


def normalize(hidden, norm_gain):
    mean_sq = jnp.mean(hidden * hidden, axis=-1, keepdims=True)
    return (hidden * lax.rsqrt(mean_sq + 1e-06) * norm_gain).astype(jnp.bfloat16)


def local(
    resid,
    q_latent,
    q_rope,
    cache_latent,
    cache_rope,
    lengths,
    w_value,
    w_out,
    norm_gain,
    routes,
    route_scores,
    placement,
    w_gate,
    w_up,
    w_down,
):
    devices = lax.axis_size("ep")
    rows_dev = resid.shape[0]
    width = resid.shape[1]
    length = cache_latent.shape[1]
    experts = placement.shape[0]
    top_count = routes.shape[1]
    cap = rows_dev * top_count // experts
    shards = devices // experts
    scale = (w_value.shape[2] + q_rope.shape[2]) ** (-0.5)
    scores = jnp.einsum("rhc,rpc->rhp", q_latent, cache_latent, preferred_element_type=jnp.float32)
    scores = scores + jnp.einsum(
        "rhk,rkp->rhp", q_rope, cache_rope, preferred_element_type=jnp.float32
    )
    scores = scores * scale
    valid = jnp.arange(length, dtype=jnp.int32)[None, None, :] < lengths[:, None, None]
    scores = jnp.where(valid, scores, -1e30)
    top = jnp.max(scores, axis=-1, keepdims=True)
    expo = jnp.where(valid, jnp.exp(scores - top), 0.0)
    probs = (expo / jnp.sum(expo, axis=-1, keepdims=True)).astype(jnp.bfloat16)
    o_local = jnp.einsum(
        "rhp,rpc->rhc", probs, cache_latent, preferred_element_type=jnp.float32
    ).astype(jnp.bfloat16)
    o_heads = lax.all_to_all(o_local, "ep", split_axis=1, concat_axis=0, tiled=True)
    values = jnp.einsum(
        "rhc,hcv->rhv", o_heads, w_value, preferred_element_type=jnp.float32
    ).astype(jnp.bfloat16)
    flat = values.reshape(values.shape[0], -1)
    expert_ids = jnp.arange(experts, dtype=jnp.int32)
    slot_of_dev = jnp.arange(devices, dtype=jnp.int32) // shards
    dev_expert = (placement[None, :] == slot_of_dev[:, None]).astype(jnp.float32)
    chosen = routes[:, :, None] == expert_ids[None, None, :]
    member = jnp.any(chosen, axis=1).astype(jnp.int32)
    weights = 2.5 * route_scores / jnp.sum(route_scores, axis=-1, keepdims=True)
    weight_expert = jnp.sum(jnp.where(chosen, weights[:, :, None], 0.0), axis=1)
    rank_rows = jnp.cumsum(member, axis=0) - member
    slots = jnp.arange(cap, dtype=jnp.int32)
    pick = (member.T[:, None, :] == 1) & (rank_rows.T[:, None, :] == slots[None, :, None])
    send_map = jnp.einsum("de,ecr->dcr", dev_expert, pick.astype(jnp.float32))
    partial = jnp.dot(flat, w_out, preferred_element_type=jnp.float32)
    partial = partial.astype(jnp.bfloat16).reshape(devices, rows_dev, width)
    shares = lax.all_to_all(partial, "ep", split_axis=0, concat_axis=0, tiled=True)
    attn = jnp.sum(shares.astype(jnp.float32), axis=0)
    hidden = resid.astype(jnp.float32) + attn
    normed = normalize(hidden, norm_gain)
    outgoing = jnp.einsum(
        "dcr,rw->dcw", send_map.astype(jnp.bfloat16), normed, preferred_element_type=jnp.float32
    ).astype(jnp.bfloat16)
    incoming = lax.all_to_all(outgoing, "ep", split_axis=0, concat_axis=0, tiled=True)
    taken = incoming.reshape(-1, width)
    dims = (((1,), (1,)), ((), ()))
    gate = lax.dot_general(taken, w_gate, dims, preferred_element_type=jnp.float32)
    up = lax.dot_general(taken, w_up, dims, preferred_element_type=jnp.float32)
    act = (jax.nn.silu(gate) * up).astype(jnp.bfloat16)
    weight_dev = jnp.dot(weight_expert, dev_expert.T, precision=lax.Precision.HIGHEST)
    combine_weights = jnp.transpose(send_map, (2, 0, 1)) * weight_dev[:, :, None]
    part_out = jnp.dot(act, w_down, preferred_element_type=jnp.float32).reshape(devices, cap, width)
    returned = lax.all_to_all(
        part_out.astype(jnp.bfloat16), "ep", split_axis=0, concat_axis=0, tiled=True
    ).astype(part_out.dtype)
    moe = jnp.einsum("rdc,dcw->rw", combine_weights, returned, precision=lax.Precision.HIGHEST)
    return (hidden + moe).astype(jnp.bfloat16)


def solution(mesh):
    return jax.shard_map(
        local,
        mesh=mesh,
        in_specs=(
            P(("groups", "ep"), None),
            P(("groups", "ep"), None, None),
            P(("groups", "ep"), None, None),
            P(("groups", "ep"), None, None),
            P(("groups", "ep"), None, None),
            P(("groups", "ep")),
            P("ep", None, None),
            P("ep", None),
            P(),
            P(("groups", "ep"), None),
            P(("groups", "ep"), None),
            P("groups"),
            P("ep", None),
            P("ep", None),
            P("ep", None),
        ),
        out_specs=P(("groups", "ep"), None),
        check_vma=False,
    )
```

```python
import functools

import jax
import jax.numpy as jnp
from jax import lax
from jax.experimental import pallas as pl
from jax.experimental.pallas import tpu as pltpu
from jax.sharding import PartitionSpec as P

F32 = jnp.float32
BF16 = jnp.bfloat16
NT = (((1,), (1,)), ((), ()))


def kernel(
    devices,
    rows_dev,
    heads_dev,
    cap,
    parts,
    scale,
    lengths_ref,
    q_latent,
    q_rope,
    resid,
    gain,
    spread,
    gather,
    cache_latent_hbm,
    cache_rope_hbm,
    w_value_hbm,
    w_out_hbm,
    w_gate_hbm,
    w_up_hbm,
    w_down_hbm,
    out,
    cache_latent,
    cache_rope,
    w_value,
    w_out,
    w_gate,
    w_up,
    w_down,
    o_wide,
    o_send,
    o_recv,
    p_wide,
    p_send,
    p_recv,
    n_send,
    n_recv,
    n_wide,
    e_wide,
    e_send,
    e_recv,
    act,
    load_sem,
    send_sem,
    recv_sem,
):
    me = lax.axis_index("ep")
    group = lax.axis_index("groups")
    loads = []
    for r in range(rows_dev):
        loads.append((cache_latent_hbm.at[r], cache_latent.at[r]))
        loads.append((cache_rope_hbm.at[r], cache_rope.at[r]))
    loads += [
        (w_value_hbm, w_value),
        (w_out_hbm, w_out),
        (w_gate_hbm, w_gate),
        (w_up_hbm, w_up),
        (w_down_hbm, w_down),
    ]
    loads = [pltpu.make_async_copy(a, b, load_sem.at[i]) for i, (a, b) in enumerate(loads)]
    for load in loads:
        load.start()

    barrier = pltpu.get_barrier_semaphore()

    @pl.loop(1, devices)
    def _(k):
        peer = lax.rem(me + k, devices)
        pl.semaphore_signal(
            barrier, inc=1, device_id=(group, peer), device_id_type=pl.DeviceIdType.MESH
        )

    def copy(phase, k, src, dst, to):
        return pltpu.make_async_remote_copy(
            src_ref=src.at[to],
            dst_ref=dst.at[me],
            send_sem=send_sem.at[phase, k],
            recv_sem=recv_sem.at[phase, k],
            device_id=(group, to),
            device_id_type=pl.DeviceIdType.MESH,
        )

    def send_all(phase, src, dst):
        @pl.loop(1, devices)
        def _(k):
            copy(phase, k, src, dst, lax.rem(me + k, devices)).start()

        dst[me] = src[me]

    def recv_all(phase, src, dst):
        @pl.loop(1, devices)
        def _(k):
            copy(phase, k, src, dst, lax.rem(me + k, devices)).wait_recv()

    def sent_all(phase, src, dst):
        @pl.loop(1, devices)
        def _(k):
            copy(phase, k, src, dst, lax.rem(me + k, devices)).wait_send()

    length, lat = cache_latent.shape[1:]
    heads = q_latent.shape[1]
    pos = lax.broadcasted_iota(jnp.int32, (heads, length), 1)
    for r in range(rows_dev):
        loads[2 * r].wait()
        loads[2 * r + 1].wait()
        keys = cache_latent[r]
        scores = lax.dot_general(q_latent[r], keys, NT, preferred_element_type=F32)
        scores = scores + jnp.dot(q_rope[r], cache_rope[r], preferred_element_type=F32)
        valid = pos < lengths_ref[r]
        scores = jnp.where(valid, scores * scale, -1e30)
        top = jnp.max(scores, axis=-1, keepdims=True)
        expo = jnp.where(valid, jnp.exp(scores - top), 0.0)
        probs = (expo / jnp.sum(expo, axis=-1, keepdims=True)).astype(BF16)
        o = jnp.dot(probs, keys, preferred_element_type=F32)
        for c in range(lat // 128):
            o_wide[:, r * (lat // 128) + c, :] = o[:, c * 128 : (c + 1) * 128]
    o_send[...] = o_wide[...].astype(BF16)
    pl.semaphore_wait(barrier, devices - 1)
    send_all(0, o_send, o_recv)

    loads[2 * rows_dev].wait()
    loads[2 * rows_dev + 1].wait()
    recv_all(0, o_send, o_recv)
    o_wide[...] = o_recv[...].astype(F32)
    steps = lat // 128
    o_all = jnp.concatenate(
        [
            jnp.concatenate([o_wide[:, r * steps + c, :] for c in range(steps)], axis=1)
            for r in range(rows_dev)
        ],
        axis=0,
    ).astype(BF16)
    values = jnp.dot(o_all, w_value[0], preferred_element_type=F32).astype(BF16)
    width = w_out.shape[1]
    piece = width // parts
    for q in range(parts):
        partial = jnp.dot(
            values, w_out[:, q * piece : (q + 1) * piece], preferred_element_type=F32
        )
        for r in range(rows_dev):
            p_wide[:, r * parts + q, :] = partial[r * devices : (r + 1) * devices, :]
    p_send[...] = p_wide[...].astype(BF16)
    send_all(1, p_send, p_recv)
    recv_all(1, p_send, p_recv)
    hidden = lax.fori_loop(
        0, devices, lambda d, total: total + p_recv[d].astype(F32), resid[...].astype(F32)
    )

    count = rows_dev * parts
    same = (
        lax.broadcasted_iota(jnp.int32, (count, count), 0) // parts
        == lax.broadcasted_iota(jnp.int32, (count, count), 1) // parts
    ).astype(F32)
    square = jnp.dot(
        same, hidden * hidden, precision=lax.Precision.HIGHEST, preferred_element_type=F32
    )
    mean_sq = jnp.sum(square, axis=-1, keepdims=True) / width
    normed = (hidden * lax.rsqrt(mean_sq + 1e-06) * gain[...]).astype(BF16)
    slot = cap * parts
    outgoing = jnp.dot(spread[...], normed, preferred_element_type=F32)
    n_send[...] = outgoing.reshape(devices, slot, piece).astype(BF16)
    send_all(2, n_send, n_recv)

    loads[2 * rows_dev + 2].wait()
    loads[2 * rows_dev + 3].wait()
    recv_all(2, n_send, n_recv)
    n_wide[...] = n_recv[...].astype(F32)
    taken = jnp.concatenate(
        [
            jnp.concatenate([n_wide[:, c * parts + q, :] for q in range(parts)], axis=1)
            for c in range(cap)
        ],
        axis=0,
    ).astype(BF16)
    units = w_gate.shape[0]
    block = min(units, 256)
    for b in range(units // block):
        at = slice(b * block, (b + 1) * block)
        gate = lax.dot_general(taken, w_gate[at, :], NT, preferred_element_type=F32)
        up = lax.dot_general(taken, w_up[at, :], NT, preferred_element_type=F32)
        act[:, at] = (gate / (1.0 + jnp.exp(-gate)) * up).astype(BF16)
    loads[2 * rows_dev + 4].wait()
    for q in range(parts):
        part = jnp.dot(act[...], w_down[:, q * piece : (q + 1) * piece], preferred_element_type=F32)
        for c in range(cap):
            e_wide[:, c * parts + q, :] = part[c * devices : (c + 1) * devices, :]
    e_send[...] = e_wide[...].astype(BF16)
    send_all(3, e_send, e_recv)
    recv_all(3, e_send, e_recv)
    returned = e_recv[...].astype(F32).reshape(devices * slot, piece)
    moe = jnp.dot(
        gather[...], returned, precision=lax.Precision.HIGHEST, preferred_element_type=F32
    )
    out[...] = (hidden + moe).astype(BF16)
    sent_all(0, o_send, o_recv)
    sent_all(1, p_send, p_recv)
    sent_all(2, n_send, n_recv)
    sent_all(3, e_send, e_recv)


def local(
    resid,
    q_latent,
    q_rope,
    cache_latent,
    cache_rope,
    lengths,
    w_value,
    w_out,
    norm_gain,
    routes,
    route_scores,
    placement,
    w_gate,
    w_up,
    w_down,
):
    devices = lax.axis_size("ep")
    rows_dev, width = resid.shape
    heads_dev, lat, vhead = w_value.shape
    experts = placement.shape[0]
    top_count = routes.shape[1]
    cap = rows_dev * top_count // experts
    shards = devices // experts
    scale = (vhead + q_rope.shape[2]) ** (-0.5)
    parts = 16 // rows_dev
    piece = width // parts
    assert heads_dev == 1 and piece % 128 == 0

    expert_ids = jnp.arange(experts, dtype=jnp.int32)
    slot_of_dev = jnp.arange(devices, dtype=jnp.int32) // shards
    dev_expert = (placement[None, :] == slot_of_dev[:, None])
    weights = 2.5 * route_scores / jnp.sum(route_scores, axis=-1, keepdims=True)
    held = jnp.any(
        (routes[:, :, None, None] == expert_ids[None, None, None, :]) & dev_expert[None, None],
        axis=3,
    )
    member = jnp.any(held, axis=1)
    weight_dev = jnp.sum(jnp.where(held, weights[:, :, None], 0.0), axis=1)
    count = member.astype(jnp.int32)
    rank = jnp.sum(
        jnp.where(
            jnp.arange(rows_dev)[:, None, None] > jnp.arange(rows_dev)[None, :, None],
            count[None],
            0,
        ),
        axis=1,
    )
    pick = member[:, :, None] & (rank[:, :, None] == jnp.arange(cap)[None, None, :])
    same = jnp.eye(parts, dtype=jnp.bool_)
    full = pick[:, None, :, :, None] & same[None, :, None, None, :]
    slot = cap * parts
    gather = jnp.where(full, weight_dev[:, None, :, None, None], 0.0).reshape(
        rows_dev * parts, devices * slot
    )
    spread = jnp.transpose(full, (2, 3, 4, 0, 1)).astype(BF16).reshape(
        devices * slot, rows_dev * parts
    )
    gain = jnp.tile(norm_gain.reshape(parts, piece), (rows_dev, 1))

    any_spec = pl.BlockSpec(memory_space=pl.ANY)
    vmem = pl.BlockSpec(memory_space=pltpu.VMEM)
    scratch = [
        pltpu.VMEM(a.shape, a.dtype)
        for a in (cache_latent, cache_rope, w_value, w_out, w_gate, w_up, w_down)
    ]
    steps = rows_dev * (lat // 128)
    o_shape = (devices, steps, 128)
    p_shape = (devices, rows_dev * parts, piece)
    n_shape = (devices, slot, piece)
    scratch += [pltpu.VMEM(o_shape, t) for t in (F32, BF16, BF16)]
    scratch += [pltpu.VMEM(p_shape, t) for t in (F32, BF16, BF16)]
    scratch += [pltpu.VMEM(n_shape, t) for t in (BF16, BF16, F32, F32, BF16, BF16)]
    scratch += [
        pltpu.VMEM((cap * devices, w_gate.shape[0]), BF16),
        pltpu.SemaphoreType.DMA((2 * rows_dev + 5,)),
        pltpu.SemaphoreType.DMA((4, devices)),
        pltpu.SemaphoreType.DMA((4, devices)),
    ]
    out = pl.pallas_call(
        functools.partial(kernel, devices, rows_dev, heads_dev, cap, parts, scale),
        out_shape=jax.ShapeDtypeStruct((rows_dev * parts, piece), BF16),
        in_specs=[pl.BlockSpec(memory_space=pltpu.SMEM)] + [vmem] * 6 + [any_spec] * 7,
        out_specs=vmem,
        scratch_shapes=scratch,
        compiler_params=pltpu.CompilerParams(
            collective_id=0, has_side_effects=True, vmem_limit_bytes=56 * 1024 * 1024
        ),
    )(
        lengths,
        q_latent,
        q_rope,
        resid.reshape(rows_dev * parts, piece),
        gain,
        spread,
        gather,
        cache_latent,
        cache_rope,
        w_value,
        w_out,
        w_gate,
        w_up,
        w_down,
    )
    return out.reshape(rows_dev, width)


def solution(mesh):
    ep = ("groups", "ep")
    return jax.shard_map(
        local,
        mesh=mesh,
        in_specs=(
            P(ep, None),
            P(ep, None, None),
            P(ep, None, None),
            P(ep, None, None),
            P(ep, None, None),
            P(ep),
            P("ep", None, None),
            P("ep", None),
            P(),
            P(ep, None),
            P(ep, None),
            P("groups"),
            P("ep", None),
            P("ep", None),
            P("ep", None),
        ),
        out_specs=P(ep, None),
        check_vma=False,
    )
```

```python
import functools

import jax
import jax.numpy as jnp
from jax import lax
from jax.experimental import pallas as pl
from jax.experimental.pallas import tpu as pltpu
from jax.sharding import PartitionSpec as P

F32 = jnp.float32
BF16 = jnp.bfloat16
NT = (((1,), (1,)), ((), ()))


def kernel(
    devices,
    rows_dev,
    cap,
    parts,
    shards,
    scale,
    lengths_ref,
    routes_ref,
    scores_ref,
    placement_ref,
    q_latent,
    q_rope,
    resid,
    norm_gain,
    cache_latent_hbm,
    cache_rope_hbm,
    w_value_hbm,
    w_out_hbm,
    w_gate_hbm,
    w_up_hbm,
    w_down_hbm,
    out,
    cache_latent,
    cache_rope,
    w_value,
    w_out,
    w_gate,
    w_up,
    w_down,
    o_wide,
    o_send,
    o_recv,
    p_wide,
    p_send,
    p_recv,
    n_send,
    n_recv,
    n_wide,
    e_wide,
    e_send,
    e_recv,
    act,
    hidden_wide,
    gain,
    final,
    load_sem,
    send_sem,
    recv_sem,
):
    me = lax.axis_index("ep")
    group = lax.axis_index("groups")
    loads = []
    for r in range(rows_dev):
        loads.append((cache_latent_hbm.at[r], cache_latent.at[r]))
        loads.append((cache_rope_hbm.at[r], cache_rope.at[r]))
    loads += [
        (w_value_hbm, w_value),
        (w_out_hbm, w_out),
        (w_gate_hbm, w_gate),
        (w_up_hbm, w_up),
        (w_down_hbm, w_down),
    ]
    loads = [pltpu.make_async_copy(a, b, load_sem.at[i]) for i, (a, b) in enumerate(loads)]
    for load in loads:
        load.start()

    barrier = pltpu.get_barrier_semaphore()

    @pl.loop(1, devices)
    def _(k):
        peer = lax.rem(me + k, devices)
        pl.semaphore_signal(
            barrier, inc=1, device_id=(group, peer), device_id_type=pl.DeviceIdType.MESH
        )

    def copy(phase, k, src, dst, to):
        return pltpu.make_async_remote_copy(
            src_ref=src.at[to],
            dst_ref=dst.at[me],
            send_sem=send_sem.at[phase, k],
            recv_sem=recv_sem.at[phase, k],
            device_id=(group, to),
            device_id_type=pl.DeviceIdType.MESH,
        )

    def send_all(phase, src, dst):
        @pl.loop(1, devices)
        def _(k):
            copy(phase, k, src, dst, lax.rem(me + k, devices)).start()

        dst[me] = src[me]

    def recv_all(phase, src, dst):
        @pl.loop(1, devices)
        def _(k):
            copy(phase, k, src, dst, lax.rem(me + k, devices)).wait_recv()

    def sent_all(phase, src, dst):
        @pl.loop(1, devices)
        def _(k):
            copy(phase, k, src, dst, lax.rem(me + k, devices)).wait_send()

    length, lat = cache_latent.shape[1:]
    heads = q_latent.shape[1]
    pos = lax.broadcasted_iota(jnp.int32, (heads, length), 1)
    for r in range(rows_dev):
        loads[2 * r].wait()
        loads[2 * r + 1].wait()
        keys = cache_latent[r]
        scores = lax.dot_general(q_latent[r], keys, NT, preferred_element_type=F32)
        scores = scores + jnp.dot(q_rope[r], cache_rope[r], preferred_element_type=F32)
        valid = pos < lengths_ref[r]
        scores = jnp.where(valid, scores * scale, -1e30)
        top = jnp.max(scores, axis=-1, keepdims=True)
        expo = jnp.where(valid, jnp.exp(scores - top), 0.0)
        probs = (expo / jnp.sum(expo, axis=-1, keepdims=True)).astype(BF16)
        o = jnp.dot(probs, keys, preferred_element_type=F32)
        for c in range(lat // 128):
            o_wide[:, r * (lat // 128) + c, :] = o[:, c * 128 : (c + 1) * 128]
    o_send[...] = o_wide[...].astype(BF16)
    pl.semaphore_wait(barrier, devices - 1)
    send_all(0, o_send, o_recv)

    width = w_out.shape[1]
    piece = width // parts
    slot = cap * parts
    wide = resid[...].astype(F32)
    for r in range(rows_dev):
        for q in range(parts):
            at = slice(q * piece, (q + 1) * piece)
            hidden_wide[r * parts + q : r * parts + q + 1, :] = wide[r : r + 1, at]
            gain[r * parts + q : r * parts + q + 1, :] = norm_gain[:, at]

    count = rows_dev * parts
    lane = lax.broadcasted_iota(jnp.int32, (count, devices * slot), 1)
    line = lax.broadcasted_iota(jnp.int32, (count, devices * slot), 0)
    row = line // parts
    holder = lane // (slot * shards)
    member = jnp.zeros(lane.shape, F32)
    rank = jnp.zeros(lane.shape, F32)
    score = jnp.zeros(lane.shape, F32)
    score_sum = jnp.zeros(lane.shape, F32)
    for r in range(rows_dev):
        for k in range(routes_ref.shape[1]):
            named = holder == placement_ref[routes_ref[r, k]]
            own = named & (row == r)
            member = member + jnp.where(own, 1.0, 0.0)
            rank = rank + jnp.where(named & (row > r), 1.0, 0.0)
            score = score + jnp.where(own, scores_ref[r, k], 0.0)
            score_sum = score_sum + jnp.where(row == r, scores_ref[r, k], 0.0)
    choice = lax.rem(lane // parts, cap).astype(F32)
    pick = (member > 0.5) & (rank == choice) & (lax.rem(lane, parts) == lax.rem(line, parts))
    gather = jnp.where(pick, 2.5 * score / score_sum, 0.0)
    spread = jnp.where(pick, 1.0, 0.0).T.astype(BF16)

    loads[2 * rows_dev].wait()
    loads[2 * rows_dev + 1].wait()
    recv_all(0, o_send, o_recv)
    o_wide[...] = o_recv[...].astype(F32)
    steps = lat // 128
    o_all = jnp.concatenate(
        [
            jnp.concatenate([o_wide[:, r * steps + c, :] for c in range(steps)], axis=1)
            for r in range(rows_dev)
        ],
        axis=0,
    ).astype(BF16)
    values = jnp.dot(o_all, w_value[0], preferred_element_type=F32).astype(BF16)
    for q in range(parts):
        partial = jnp.dot(
            values, w_out[:, q * piece : (q + 1) * piece], preferred_element_type=F32
        )
        for r in range(rows_dev):
            p_wide[:, r * parts + q, :] = partial[r * devices : (r + 1) * devices, :]
    p_send[...] = p_wide[...].astype(BF16)
    send_all(1, p_send, p_recv)
    recv_all(1, p_send, p_recv)
    hidden = lax.fori_loop(
        0, devices, lambda d, total: total + p_recv[d].astype(F32), hidden_wide[...]
    )

    same = (
        lax.broadcasted_iota(jnp.int32, (count, count), 0) // parts
        == lax.broadcasted_iota(jnp.int32, (count, count), 1) // parts
    ).astype(F32)
    square = jnp.dot(
        same, hidden * hidden, precision=lax.Precision.HIGHEST, preferred_element_type=F32
    )
    mean_sq = jnp.sum(square, axis=-1, keepdims=True) / width
    normed = (hidden * lax.rsqrt(mean_sq + 1e-06) * gain[...]).astype(BF16)
    outgoing = jnp.dot(spread, normed, preferred_element_type=F32)
    n_send[...] = outgoing.reshape(devices, slot, piece).astype(BF16)
    send_all(2, n_send, n_recv)

    loads[2 * rows_dev + 2].wait()
    loads[2 * rows_dev + 3].wait()
    recv_all(2, n_send, n_recv)
    n_wide[...] = n_recv[...].astype(F32)
    taken = jnp.concatenate(
        [
            jnp.concatenate([n_wide[:, c * parts + q, :] for q in range(parts)], axis=1)
            for c in range(cap)
        ],
        axis=0,
    ).astype(BF16)
    units = w_gate.shape[0]
    block = min(units, 256)
    for b in range(units // block):
        at = slice(b * block, (b + 1) * block)
        gate = lax.dot_general(taken, w_gate[at, :], NT, preferred_element_type=F32)
        up = lax.dot_general(taken, w_up[at, :], NT, preferred_element_type=F32)
        act[:, at] = (gate / (1.0 + jnp.exp(-gate)) * up).astype(BF16)
    loads[2 * rows_dev + 4].wait()
    for q in range(parts):
        part = jnp.dot(act[...], w_down[:, q * piece : (q + 1) * piece], preferred_element_type=F32)
        for c in range(cap):
            e_wide[:, c * parts + q, :] = part[c * devices : (c + 1) * devices, :]
    e_send[...] = e_wide[...].astype(BF16)
    send_all(3, e_send, e_recv)
    recv_all(3, e_send, e_recv)
    returned = e_recv[...].astype(F32).reshape(devices * slot, piece)
    moe = jnp.dot(
        gather, returned, precision=lax.Precision.HIGHEST, preferred_element_type=F32
    )
    mixed = hidden + moe
    for r in range(rows_dev):
        for q in range(parts):
            final[r : r + 1, q * piece : (q + 1) * piece] = mixed[r * parts + q : r * parts + q + 1, :]
    out[...] = final[...].astype(BF16)
    sent_all(0, o_send, o_recv)
    sent_all(1, p_send, p_recv)
    sent_all(2, n_send, n_recv)
    sent_all(3, e_send, e_recv)


def local(
    resid,
    q_latent,
    q_rope,
    cache_latent,
    cache_rope,
    lengths,
    w_value,
    w_out,
    norm_gain,
    routes,
    route_scores,
    placement,
    w_gate,
    w_up,
    w_down,
):
    devices = lax.axis_size("ep")
    rows_dev, width = resid.shape
    heads_dev, lat, vhead = w_value.shape
    experts = placement.shape[0]
    top_count = routes.shape[1]
    cap = rows_dev * top_count // experts
    shards = devices // experts
    scale = (vhead + q_rope.shape[2]) ** (-0.5)
    parts = 16 // rows_dev
    piece = width // parts
    assert heads_dev == 1 and piece % 128 == 0

    slot = cap * parts
    any_spec = pl.BlockSpec(memory_space=pl.ANY)
    vmem = pl.BlockSpec(memory_space=pltpu.VMEM)
    scratch = [
        pltpu.VMEM(a.shape, a.dtype)
        for a in (cache_latent, cache_rope, w_value, w_out, w_gate, w_up, w_down)
    ]
    steps = rows_dev * (lat // 128)
    o_shape = (devices, steps, 128)
    p_shape = (devices, rows_dev * parts, piece)
    n_shape = (devices, slot, piece)
    scratch += [pltpu.VMEM(o_shape, t) for t in (F32, BF16, BF16)]
    scratch += [pltpu.VMEM(p_shape, t) for t in (F32, BF16, BF16)]
    scratch += [pltpu.VMEM(n_shape, t) for t in (BF16, BF16, F32, F32, BF16, BF16)]
    scratch += [
        pltpu.VMEM((cap * devices, w_gate.shape[0]), BF16),
        pltpu.VMEM((rows_dev * parts, piece), F32),
        pltpu.VMEM((rows_dev * parts, piece), F32),
        pltpu.VMEM((rows_dev, width), F32),
        pltpu.SemaphoreType.DMA((2 * rows_dev + 5,)),
        pltpu.SemaphoreType.DMA((4, devices)),
        pltpu.SemaphoreType.DMA((4, devices)),
    ]
    out = pl.pallas_call(
        functools.partial(kernel, devices, rows_dev, cap, parts, shards, scale),
        out_shape=jax.ShapeDtypeStruct((rows_dev, width), BF16),
        in_specs=[pl.BlockSpec(memory_space=pltpu.SMEM)] * 4 + [vmem] * 4 + [any_spec] * 7,
        out_specs=vmem,
        scratch_shapes=scratch,
        compiler_params=pltpu.CompilerParams(
            collective_id=0, has_side_effects=True, vmem_limit_bytes=56 * 1024 * 1024
        ),
    )(
        lengths,
        routes,
        route_scores,
        placement,
        q_latent,
        q_rope,
        resid,
        norm_gain.reshape(1, width),
        cache_latent,
        cache_rope,
        w_value,
        w_out,
        w_gate,
        w_up,
        w_down,
    )
    return out


def solution(mesh):
    ep = ("groups", "ep")
    return jax.shard_map(
        local,
        mesh=mesh,
        in_specs=(
            P(ep, None),
            P(ep, None, None),
            P(ep, None, None),
            P(ep, None, None),
            P(ep, None, None),
            P(ep),
            P("ep", None, None),
            P("ep", None),
            P(),
            P(ep, None),
            P(ep, None),
            P("groups"),
            P("ep", None),
            P("ep", None),
            P("ep", None),
        ),
        out_specs=P(ep, None),
        check_vma=False,
    )
```

```python
import functools

import jax
import jax.numpy as jnp
from jax import lax
from jax.experimental import pallas as pl
from jax.experimental.pallas import tpu as pltpu
from jax.sharding import PartitionSpec as P

F32 = jnp.float32
BF16 = jnp.bfloat16
NT = (((1,), (1,)), ((), ()))


def kernel(
    devices,
    rows_dev,
    cap,
    parts,
    shards,
    scale,
    lengths_ref,
    routes_ref,
    scores_ref,
    placement_ref,
    q_latent,
    q_rope,
    resid,
    norm_gain,
    cache_latent_hbm,
    cache_rope_hbm,
    w_value_hbm,
    w_out_hbm,
    w_gate_hbm,
    w_up_hbm,
    w_down_hbm,
    out,
    cache_latent,
    cache_rope,
    w_value,
    w_out,
    w_gate,
    w_up,
    w_down,
    o_wide,
    o_send,
    o_recv,
    p_wide,
    p_send,
    q_recv,
    s_send,
    p_recv,
    n_send,
    n_recv,
    n_wide,
    e_wide,
    e_send,
    e_recv,
    act,
    hidden_wide,
    gain,
    final,
    load_sem,
    send_sem,
    recv_sem,
):
    me = lax.axis_index("ep")
    group = lax.axis_index("groups")
    loads = []
    for r in range(rows_dev):
        loads.append((cache_latent_hbm.at[r], cache_latent.at[r]))
        loads.append((cache_rope_hbm.at[r], cache_rope.at[r]))
    loads += [
        (w_value_hbm, w_value),
        (w_out_hbm, w_out),
        (w_gate_hbm, w_gate),
        (w_up_hbm, w_up),
        (w_down_hbm, w_down),
    ]
    loads = [pltpu.make_async_copy(a, b, load_sem.at[i]) for i, (a, b) in enumerate(loads)]
    early = 2 * rows_dev + 2
    for load in loads[:early]:
        load.start()

    barrier = pltpu.get_barrier_semaphore()

    chips = devices // 2
    core = lax.rem(me, 2)
    chip = me // 2

    def peer_of(k):
        peer, bit = 0, 1
        while bit < devices:
            mine, other = lax.rem(me // bit, 2), lax.rem(k // bit, 2)
            peer = peer + bit * (mine + other - 2 * mine * other)
            bit *= 2
        return peer

    @pl.loop(1, devices)
    def _(k):
        pl.semaphore_signal(
            barrier, inc=1, device_id=(group, peer_of(k)), device_id_type=pl.DeviceIdType.MESH
        )

    def copy(phase, k, src, dst, to):
        return pltpu.make_async_remote_copy(
            src_ref=src,
            dst_ref=dst,
            send_sem=send_sem.at[phase, k],
            recv_sem=recv_sem.at[phase, k],
            device_id=(group, to),
            device_id_type=pl.DeviceIdType.MESH,
        )

    by_core = core * chips + chip

    def exchange(phase, act_on):
        @pl.loop(0, (chips if phase == 1 else devices) - 1)
        def _(j):
            if phase == 1:
                k = devices - 2 - 2 * j
            else:
                k = devices - 1 - j
            to = peer_of(k)
            if phase == 0:
                pair = o_send.at[to], o_recv.at[by_core]
            elif phase == 1:
                pair = s_send.at[to // 2], p_recv.at[chip]
            elif phase == 2:
                pair = n_send.at[to], n_recv.at[me]
            else:
                pair = e_send.at[to], e_recv.at[me]
            act_on(copy(phase, k, *pair, to))

    def send_all(phase):
        exchange(phase, lambda c: c.start())

    def recv_all(phase):
        exchange(phase, lambda c: c.wait_recv())

    def sent_all(phase):
        exchange(phase, lambda c: c.wait_send())

    length, lat = cache_latent.shape[1:]
    heads = q_latent.shape[1]
    pos = lax.broadcasted_iota(jnp.int32, (heads, length), 1)
    for r in range(rows_dev):
        loads[2 * r].wait()
        loads[2 * r + 1].wait()
        if r == rows_dev - 1:
            for load in loads[early:]:
                load.start()
        keys = cache_latent[r]
        scores = lax.dot_general(q_latent[r], keys, NT, preferred_element_type=F32)
        scores = scores + jnp.dot(q_rope[r], cache_rope[r], preferred_element_type=F32)
        valid = pos < lengths_ref[r]
        scores = jnp.where(valid, scores * scale, -1e30)
        top = jnp.max(scores, axis=-1, keepdims=True)
        expo = jnp.where(valid, jnp.exp(scores - top), 0.0)
        probs = (expo / jnp.sum(expo, axis=-1, keepdims=True)).astype(BF16)
        o = jnp.dot(probs, keys, preferred_element_type=F32)
        for c in range(lat // 128):
            o_wide[:, r * (lat // 128) + c, :] = o[:, c * 128 : (c + 1) * 128]
    o_send[...] = o_wide[...].astype(BF16)
    pl.semaphore_wait(barrier, devices - 1)
    send_all(0)
    o_recv[by_core] = o_send[me]

    width = w_out.shape[1]
    piece = width // parts
    slot = cap * parts
    wide = resid[...].astype(F32)
    for r in range(rows_dev):
        for q in range(parts):
            at = slice(q * piece, (q + 1) * piece)
            hidden_wide[r * parts + q : r * parts + q + 1, :] = wide[r : r + 1, at]
            gain[r * parts + q : r * parts + q + 1, :] = norm_gain[:, at]

    count = rows_dev * parts
    lane = lax.broadcasted_iota(jnp.int32, (count, devices * slot), 1)
    line = lax.broadcasted_iota(jnp.int32, (count, devices * slot), 0)
    row = line // parts
    holder = lane // (slot * shards)
    member = jnp.zeros(lane.shape, F32)
    rank = jnp.zeros(lane.shape, F32)
    score = jnp.zeros(lane.shape, F32)
    score_sum = jnp.zeros(lane.shape, F32)
    for r in range(rows_dev):
        for k in range(routes_ref.shape[1]):
            named = holder == placement_ref[routes_ref[r, k]]
            own = named & (row == r)
            member = member + jnp.where(own, 1.0, 0.0)
            rank = rank + jnp.where(named & (row > r), 1.0, 0.0)
            score = score + jnp.where(own, scores_ref[r, k], 0.0)
            score_sum = score_sum + jnp.where(row == r, scores_ref[r, k], 0.0)
    choice = lax.rem(lane // parts, cap).astype(F32)
    pick = (member > 0.5) & (rank == choice) & (lax.rem(lane, parts) == lax.rem(line, parts))
    gather = jnp.where(pick, 2.5 * score / score_sum, 0.0)
    spread = jnp.where(pick, 1.0, 0.0).T.astype(BF16)

    loads[2 * rows_dev].wait()
    loads[2 * rows_dev + 1].wait()
    recv_all(0)
    o_wide[...] = o_recv[...].astype(F32)
    steps = lat // 128
    o_all = jnp.concatenate(
        [
            jnp.concatenate([o_wide[:, r * steps + c, :] for c in range(steps)], axis=1)
            for r in range(rows_dev)
        ],
        axis=0,
    ).astype(BF16)
    values = jnp.dot(o_all, w_value[0], preferred_element_type=F32).astype(BF16)
    for q in range(parts):
        partial = jnp.dot(
            values, w_out[:, q * piece : (q + 1) * piece], preferred_element_type=F32
        )
        for r in range(rows_dev):
            p_wide[:, r * parts + q, :] = partial[r * devices : (r + 1) * devices, :]
    p_send[...] = p_wide[pl.ds((1 - core) * chips, chips)].astype(BF16)
    swap = copy(4, 1, p_send, q_recv, me + 1 - 2 * core)
    swap.start()
    swap.wait_recv()

    @pl.loop(0, chips)
    def _(c):
        s_send[c] = (p_wide[core * chips + c] + q_recv[c].astype(F32)).astype(BF16)

    send_all(1)
    p_recv[chip] = s_send[chip]
    recv_all(1)
    hidden = lax.fori_loop(
        0, chips, lambda d, total: total + p_recv[d].astype(F32), hidden_wide[...]
    )

    same = (
        lax.broadcasted_iota(jnp.int32, (count, count), 0) // parts
        == lax.broadcasted_iota(jnp.int32, (count, count), 1) // parts
    ).astype(F32)
    square = jnp.dot(
        same, hidden * hidden, precision=lax.Precision.HIGHEST, preferred_element_type=F32
    )
    mean_sq = jnp.sum(square, axis=-1, keepdims=True) / width
    normed = (hidden * lax.rsqrt(mean_sq + 1e-06) * gain[...]).astype(BF16)
    outgoing = jnp.dot(spread, normed, preferred_element_type=F32)
    n_send[...] = outgoing.reshape(devices, slot, piece).astype(BF16)
    send_all(2)
    n_recv[me] = n_send[me]

    loads[2 * rows_dev + 2].wait()
    loads[2 * rows_dev + 3].wait()
    recv_all(2)
    n_wide[...] = n_recv[...].astype(F32)
    taken = jnp.concatenate(
        [
            jnp.concatenate([n_wide[:, c * parts + q, :] for q in range(parts)], axis=1)
            for c in range(cap)
        ],
        axis=0,
    ).astype(BF16)
    units = w_gate.shape[0]
    block = min(units, 256)
    for b in range(units // block):
        at = slice(b * block, (b + 1) * block)
        gate = lax.dot_general(taken, w_gate[at, :], NT, preferred_element_type=F32)
        up = lax.dot_general(taken, w_up[at, :], NT, preferred_element_type=F32)
        act[:, at] = (gate / (1.0 + jnp.exp(-gate)) * up).astype(BF16)
    loads[2 * rows_dev + 4].wait()
    for q in range(parts):
        part = jnp.dot(act[...], w_down[:, q * piece : (q + 1) * piece], preferred_element_type=F32)
        for c in range(cap):
            e_wide[:, c * parts + q, :] = part[c * devices : (c + 1) * devices, :]
    e_send[...] = e_wide[...].astype(BF16)
    send_all(3)
    e_recv[me] = e_send[me]
    recv_all(3)
    returned = e_recv[...].astype(F32).reshape(devices * slot, piece)
    moe = jnp.dot(
        gather, returned, precision=lax.Precision.HIGHEST, preferred_element_type=F32
    )
    mixed = hidden + moe
    for r in range(rows_dev):
        for q in range(parts):
            final[r : r + 1, q * piece : (q + 1) * piece] = mixed[r * parts + q : r * parts + q + 1, :]
    out[...] = final[...].astype(BF16)
    swap.wait_send()
    for phase in range(4):
        sent_all(phase)


def local(
    resid,
    q_latent,
    q_rope,
    cache_latent,
    cache_rope,
    lengths,
    w_value,
    w_out,
    norm_gain,
    routes,
    route_scores,
    placement,
    w_gate,
    w_up,
    w_down,
):
    devices = lax.axis_size("ep")
    rows_dev, width = resid.shape
    heads_dev, lat, vhead = w_value.shape
    experts = placement.shape[0]
    top_count = routes.shape[1]
    cap = rows_dev * top_count // experts
    shards = devices // experts
    scale = (vhead + q_rope.shape[2]) ** (-0.5)
    parts = 16 // rows_dev
    piece = width // parts
    assert heads_dev == 1 and piece % 128 == 0 and devices & (devices - 1) == 0

    slot = cap * parts
    any_spec = pl.BlockSpec(memory_space=pl.ANY)
    vmem = pl.BlockSpec(memory_space=pltpu.VMEM)
    scratch = [
        pltpu.VMEM(a.shape, a.dtype)
        for a in (cache_latent, cache_rope, w_value, w_out, w_gate, w_up, w_down)
    ]
    steps = rows_dev * (lat // 128)
    o_shape = (devices, steps, 128)
    p_shape = (devices, rows_dev * parts, piece)
    n_shape = (devices, slot, piece)
    scratch += [pltpu.VMEM(o_shape, t) for t in (F32, BF16, BF16)]
    scratch += [pltpu.VMEM(p_shape, F32)]
    scratch += [pltpu.VMEM((devices // 2,) + p_shape[1:], BF16)] * 4
    scratch += [pltpu.VMEM(n_shape, t) for t in (BF16, BF16, F32, F32, BF16, BF16)]
    scratch += [
        pltpu.VMEM((cap * devices, w_gate.shape[0]), BF16),
        pltpu.VMEM((rows_dev * parts, piece), F32),
        pltpu.VMEM((rows_dev * parts, piece), F32),
        pltpu.VMEM((rows_dev, width), F32),
        pltpu.SemaphoreType.DMA((2 * rows_dev + 5,)),
        pltpu.SemaphoreType.DMA((5, devices)),
        pltpu.SemaphoreType.DMA((5, devices)),
    ]
    out = pl.pallas_call(
        functools.partial(kernel, devices, rows_dev, cap, parts, shards, scale),
        out_shape=jax.ShapeDtypeStruct((rows_dev, width), BF16),
        in_specs=[pl.BlockSpec(memory_space=pltpu.SMEM)] * 4 + [vmem] * 4 + [any_spec] * 7,
        out_specs=vmem,
        scratch_shapes=scratch,
        compiler_params=pltpu.CompilerParams(
            collective_id=0, has_side_effects=True, vmem_limit_bytes=56 * 1024 * 1024
        ),
    )(
        lengths,
        routes,
        route_scores,
        placement,
        q_latent,
        q_rope,
        resid,
        norm_gain.reshape(1, width),
        cache_latent,
        cache_rope,
        w_value,
        w_out,
        w_gate,
        w_up,
        w_down,
    )
    return out


def solution(mesh):
    ep = ("groups", "ep")
    return jax.shard_map(
        local,
        mesh=mesh,
        in_specs=(
            P(ep, None),
            P(ep, None, None),
            P(ep, None, None),
            P(ep, None, None),
            P(ep, None, None),
            P(ep),
            P("ep", None, None),
            P("ep", None),
            P(),
            P(ep, None),
            P(ep, None),
            P("groups"),
            P("ep", None),
            P("ep", None),
            P("ep", None),
        ),
        out_specs=P(ep, None),
        check_vma=False,
    )
```

```python
import functools

import jax
import jax.numpy as jnp
from jax import lax
from jax.experimental import pallas as pl
from jax.experimental.pallas import tpu as pltpu
from jax.sharding import PartitionSpec as P

F32 = jnp.float32
BF16 = jnp.bfloat16
NT = (((1,), (1,)), ((), ()))


def kernel(
    devices,
    rows_dev,
    cap,
    parts,
    shards,
    scale,
    lengths_ref,
    routes_ref,
    scores_ref,
    placement_ref,
    q_latent,
    q_rope,
    resid,
    norm_gain,
    cache_latent_hbm,
    cache_rope_hbm,
    w_value_hbm,
    w_out_hbm,
    w_gate_hbm,
    w_up_hbm,
    w_down_hbm,
    out,
    cache_latent,
    cache_rope,
    w_value,
    w_out,
    w_gate,
    w_up,
    w_down,
    o_wide,
    o_send,
    o_recv,
    p_wide,
    p_send,
    q_recv,
    s_send,
    p_recv,
    n_send,
    n_recv,
    n_wide,
    e_wide,
    e_send,
    e_recv,
    act,
    hidden_wide,
    gain,
    final,
    load_sem,
    send_sem,
    recv_sem,
):
    me = lax.axis_index("ep")
    group = lax.axis_index("groups")
    loads = []
    for r in range(rows_dev):
        loads.append((cache_latent_hbm.at[r], cache_latent.at[r]))
        loads.append((cache_rope_hbm.at[r], cache_rope.at[r]))
    loads += [
        (w_value_hbm, w_value),
        (w_out_hbm, w_out),
        (w_gate_hbm, w_gate),
        (w_up_hbm, w_up),
        (w_down_hbm, w_down),
    ]
    loads = [pltpu.make_async_copy(a, b, load_sem.at[i]) for i, (a, b) in enumerate(loads)]
    early = 2 * rows_dev + 2
    for load in loads[:early]:
        load.start()

    barrier = pltpu.get_barrier_semaphore()

    chips = devices // 2
    core = lax.rem(me, 2)
    chip = me // 2

    def peer_of(k):
        peer, bit = 0, 1
        while bit < devices:
            mine, other = lax.rem(me // bit, 2), lax.rem(k // bit, 2)
            peer = peer + bit * (mine + other - 2 * mine * other)
            bit *= 2
        return peer

    @pl.loop(1, devices)
    def _(k):
        pl.semaphore_signal(
            barrier, inc=1, device_id=(group, peer_of(k)), device_id_type=pl.DeviceIdType.MESH
        )

    def copy(phase, k, src, dst, to):
        return pltpu.make_async_remote_copy(
            src_ref=src,
            dst_ref=dst,
            send_sem=send_sem.at[phase, k],
            recv_sem=recv_sem.at[phase, k],
            device_id=(group, to),
            device_id_type=pl.DeviceIdType.MESH,
        )

    by_core = core * chips + chip

    def exchange(phase, act_on, make=None):
        @pl.loop(0, (chips if phase == 1 else devices) - 1, unroll=devices <= 16)
        def _(j):
            if phase == 1:
                k = devices - 2 - 2 * j
            else:
                k = devices - 1 - j
            to = peer_of(k)
            if phase == 0:
                pair = o_send.at[to], o_recv.at[by_core]
            elif phase == 1:
                pair = s_send.at[to // 2], p_recv.at[chip]
            elif phase == 2:
                pair = n_send.at[to], n_recv.at[me]
            else:
                pair = e_send.at[to], e_recv.at[me]
            if make is not None:
                make(to // 2 if phase == 1 else to)
            act_on(copy(phase, k, *pair, to))

    def send_all(phase, make):
        exchange(phase, lambda c: c.start(), make)
        make(chip if phase == 1 else me)

    def recv_all(phase):
        exchange(phase, lambda c: c.wait_recv())

    def sent_all(phase):
        exchange(phase, lambda c: c.wait_send())

    length, lat = cache_latent.shape[1:]
    heads = q_latent.shape[1]
    pos = lax.broadcasted_iota(jnp.int32, (heads, length), 1)
    for r in range(rows_dev):
        loads[2 * r].wait()
        loads[2 * r + 1].wait()
        if r == rows_dev - 1:
            for load in loads[early:]:
                load.start()
        keys = cache_latent[r]
        scores = lax.dot_general(q_latent[r], keys, NT, preferred_element_type=F32)
        scores = scores + jnp.dot(q_rope[r], cache_rope[r], preferred_element_type=F32)
        valid = pos < lengths_ref[r]
        scores = jnp.where(valid, scores * scale, -1e30)
        top = jnp.max(scores, axis=-1, keepdims=True)
        expo = jnp.where(valid, jnp.exp(scores - top), 0.0)
        probs = (expo / jnp.sum(expo, axis=-1, keepdims=True)).astype(BF16)
        o = jnp.dot(probs, keys, preferred_element_type=F32)
        for c in range(lat // 128):
            o_wide[:, r * (lat // 128) + c, :] = o[:, c * 128 : (c + 1) * 128]

    def make_o(d):
        o_send[d] = o_wide[d].astype(BF16)

    pl.semaphore_wait(barrier, devices - 1)
    send_all(0, make_o)
    o_recv[by_core] = o_send[me]

    width = w_out.shape[1]
    piece = width // parts
    slot = cap * parts
    wide = resid[...].astype(F32)
    for r in range(rows_dev):
        for q in range(parts):
            at = slice(q * piece, (q + 1) * piece)
            hidden_wide[r * parts + q : r * parts + q + 1, :] = wide[r : r + 1, at]
            gain[r * parts + q : r * parts + q + 1, :] = norm_gain[:, at]

    count = rows_dev * parts
    lane = lax.broadcasted_iota(jnp.int32, (count, devices * slot), 1)
    line = lax.broadcasted_iota(jnp.int32, (count, devices * slot), 0)
    row = line // parts
    holder = lane // (slot * shards)
    member = jnp.zeros(lane.shape, F32)
    rank = jnp.zeros(lane.shape, F32)
    score = jnp.zeros(lane.shape, F32)
    score_sum = jnp.zeros(lane.shape, F32)
    for r in range(rows_dev):
        for k in range(routes_ref.shape[1]):
            named = holder == placement_ref[routes_ref[r, k]]
            own = named & (row == r)
            member = member + jnp.where(own, 1.0, 0.0)
            rank = rank + jnp.where(named & (row > r), 1.0, 0.0)
            score = score + jnp.where(own, scores_ref[r, k], 0.0)
            score_sum = score_sum + jnp.where(row == r, scores_ref[r, k], 0.0)
    choice = lax.rem(lane // parts, cap).astype(F32)
    pick = (member > 0.5) & (rank == choice) & (lax.rem(lane, parts) == lax.rem(line, parts))
    gather = jnp.where(pick, 2.5 * score / score_sum, 0.0)
    spread = jnp.where(pick, 1.0, 0.0).T.astype(BF16)

    loads[2 * rows_dev].wait()
    loads[2 * rows_dev + 1].wait()
    recv_all(0)
    o_wide[...] = o_recv[...].astype(F32)
    steps = lat // 128
    o_all = jnp.concatenate(
        [
            jnp.concatenate([o_wide[:, r * steps + c, :] for c in range(steps)], axis=1)
            for r in range(rows_dev)
        ],
        axis=0,
    ).astype(BF16)
    values = jnp.dot(o_all, w_value[0], preferred_element_type=F32).astype(BF16)
    for q in range(parts):
        partial = jnp.dot(
            values, w_out[:, q * piece : (q + 1) * piece], preferred_element_type=F32
        )
        for r in range(rows_dev):
            p_wide[:, r * parts + q, :] = partial[r * devices : (r + 1) * devices, :]
    p_send[...] = p_wide[pl.ds((1 - core) * chips, chips)].astype(BF16)
    swap = copy(4, 1, p_send, q_recv, me + 1 - 2 * core)
    swap.start()
    swap.wait_recv()

    def make_s(c):
        s_send[c] = (p_wide[core * chips + c] + q_recv[c].astype(F32)).astype(BF16)

    send_all(1, make_s)
    p_recv[chip] = s_send[chip]
    recv_all(1)
    hidden = lax.fori_loop(
        0, chips, lambda d, total: total + p_recv[d].astype(F32), hidden_wide[...]
    )

    same = (
        lax.broadcasted_iota(jnp.int32, (count, count), 0) // parts
        == lax.broadcasted_iota(jnp.int32, (count, count), 1) // parts
    ).astype(F32)
    square = jnp.dot(
        same, hidden * hidden, precision=lax.Precision.HIGHEST, preferred_element_type=F32
    )
    mean_sq = jnp.sum(square, axis=-1, keepdims=True) / width
    normed = (hidden * lax.rsqrt(mean_sq + 1e-06) * gain[...]).astype(BF16)
    outgoing = jnp.dot(spread, normed, preferred_element_type=F32)
    n_wide[...] = outgoing.reshape(devices, slot, piece)

    def make_n(d):
        n_send[d] = n_wide[d].astype(BF16)

    send_all(2, make_n)
    n_recv[me] = n_send[me]

    loads[2 * rows_dev + 2].wait()
    loads[2 * rows_dev + 3].wait()
    recv_all(2)
    n_wide[...] = n_recv[...].astype(F32)
    taken = jnp.concatenate(
        [
            jnp.concatenate([n_wide[:, c * parts + q, :] for q in range(parts)], axis=1)
            for c in range(cap)
        ],
        axis=0,
    ).astype(BF16)
    units = w_gate.shape[0]
    block = min(units, 256)
    for b in range(units // block):
        at = slice(b * block, (b + 1) * block)
        gate = lax.dot_general(taken, w_gate[at, :], NT, preferred_element_type=F32)
        up = lax.dot_general(taken, w_up[at, :], NT, preferred_element_type=F32)
        act[:, at] = (gate / (1.0 + jnp.exp(-gate)) * up).astype(BF16)
    loads[2 * rows_dev + 4].wait()
    for q in range(parts):
        part = jnp.dot(act[...], w_down[:, q * piece : (q + 1) * piece], preferred_element_type=F32)
        for c in range(cap):
            e_wide[:, c * parts + q, :] = part[c * devices : (c + 1) * devices, :]

    def make_e(d):
        e_send[d] = e_wide[d].astype(BF16)

    send_all(3, make_e)
    e_recv[me] = e_send[me]
    recv_all(3)
    returned = e_recv[...].astype(F32).reshape(devices * slot, piece)
    moe = jnp.dot(
        gather, returned, precision=lax.Precision.HIGHEST, preferred_element_type=F32
    )
    mixed = hidden + moe
    for r in range(rows_dev):
        for q in range(parts):
            final[r : r + 1, q * piece : (q + 1) * piece] = mixed[r * parts + q : r * parts + q + 1, :]
    out[...] = final[...].astype(BF16)
    swap.wait_send()
    for phase in range(4):
        sent_all(phase)


def local(
    resid,
    q_latent,
    q_rope,
    cache_latent,
    cache_rope,
    lengths,
    w_value,
    w_out,
    norm_gain,
    routes,
    route_scores,
    placement,
    w_gate,
    w_up,
    w_down,
):
    devices = lax.axis_size("ep")
    rows_dev, width = resid.shape
    heads_dev, lat, vhead = w_value.shape
    experts = placement.shape[0]
    top_count = routes.shape[1]
    cap = rows_dev * top_count // experts
    shards = devices // experts
    scale = (vhead + q_rope.shape[2]) ** (-0.5)
    parts = 16 // rows_dev
    piece = width // parts
    assert heads_dev == 1 and piece % 128 == 0 and devices & (devices - 1) == 0

    slot = cap * parts
    any_spec = pl.BlockSpec(memory_space=pl.ANY)
    vmem = pl.BlockSpec(memory_space=pltpu.VMEM)
    scratch = [
        pltpu.VMEM(a.shape, a.dtype)
        for a in (cache_latent, cache_rope, w_value, w_out, w_gate, w_up, w_down)
    ]
    steps = rows_dev * (lat // 128)
    o_shape = (devices, steps, 128)
    p_shape = (devices, rows_dev * parts, piece)
    n_shape = (devices, slot, piece)
    scratch += [pltpu.VMEM(o_shape, t) for t in (F32, BF16, BF16)]
    scratch += [pltpu.VMEM(p_shape, F32)]
    scratch += [pltpu.VMEM((devices // 2,) + p_shape[1:], BF16)] * 4
    scratch += [pltpu.VMEM(n_shape, t) for t in (BF16, BF16, F32, F32, BF16, BF16)]
    scratch += [
        pltpu.VMEM((cap * devices, w_gate.shape[0]), BF16),
        pltpu.VMEM((rows_dev * parts, piece), F32),
        pltpu.VMEM((rows_dev * parts, piece), F32),
        pltpu.VMEM((rows_dev, width), F32),
        pltpu.SemaphoreType.DMA((2 * rows_dev + 5,)),
        pltpu.SemaphoreType.DMA((5, devices)),
        pltpu.SemaphoreType.DMA((5, devices)),
    ]
    out = pl.pallas_call(
        functools.partial(kernel, devices, rows_dev, cap, parts, shards, scale),
        out_shape=jax.ShapeDtypeStruct((rows_dev, width), BF16),
        in_specs=[pl.BlockSpec(memory_space=pltpu.SMEM)] * 4 + [vmem] * 4 + [any_spec] * 7,
        out_specs=vmem,
        scratch_shapes=scratch,
        compiler_params=pltpu.CompilerParams(
            collective_id=0, has_side_effects=True, vmem_limit_bytes=56 * 1024 * 1024
        ),
    )(
        lengths,
        routes,
        route_scores,
        placement,
        q_latent,
        q_rope,
        resid,
        norm_gain.reshape(1, width),
        cache_latent,
        cache_rope,
        w_value,
        w_out,
        w_gate,
        w_up,
        w_down,
    )
    return out


def solution(mesh):
    ep = ("groups", "ep")
    return jax.shard_map(
        local,
        mesh=mesh,
        in_specs=(
            P(ep, None),
            P(ep, None, None),
            P(ep, None, None),
            P(ep, None, None),
            P(ep, None, None),
            P(ep),
            P("ep", None, None),
            P("ep", None),
            P(),
            P(ep, None),
            P(ep, None),
            P("groups"),
            P("ep", None),
            P("ep", None),
            P("ep", None),
        ),
        out_specs=P(ep, None),
        check_vma=False,
    )
```
